32 devices in a mesh: blocks: 2 (over x), gz: 8 (over z, y), ta: 2 (over core).
Axes of the slice: x: 2, y: 2, z: 4, core: 2. Of those that a mesh axis runs over, the one named last changes fastest.
Arguments:
- field: float32 [4, 512, 256, 512], P(('blocks', 'ta'), 'gz'), parts along dimension 0, may hold values from -13 to 13
- start_x: float32 [512, 64], replicated, may hold values from -6 to 6
- start_z: float32 [512, 64], replicated, may hold values from -6 to 6
Outputs:
- core: float32 [128, 2, 64, 256], P(('blocks', 'gz'), 'ta'), parts along dimension 0
- basis_x: float32 [1024, 64], P('blocks'), parts along dimension 0
- basis_z: float32 [1024, 64], P('blocks'), parts along dimension 0
The draws below stay inside these ranges and needn't reach their ends.
There are 2 independent parts, one for each index of `blocks`. The reference program is written for one: setup_inputs(seed, part) draws one part's arguments, and reference() takes and returns one part's arrays. A program takes and returns all parts, laid end to end along the dimension named above; an argument that names none is the same for every part. Nothing has to cross between parts.
All inputs are finite; a program needn't handle non-finite values.
Results may differ from the reference program's by a relative error of at most 0.00026.
Values sent between devices are 32-bit elements; how exact they have to be, the bound alone decides.
A program may use at most 128 MiB of HBM per device.

```python
import math
import jax
import jax.numpy as jnp
from jax import lax

N1 = 512
N2 = 256
N3 = 512
NT = 2
R1 = 64
R3 = 64
SWEEPS = 3


def draw_field(key, part):
    key = jax.random.fold_in(key, 11)
    key_scale, key_noise = jax.random.split(key)
    spread = math.log(3.16)
    noise = jnp.clip(jax.random.normal(key_noise, (NT, N3, N2, N1), jnp.float32), -4.0, 4.0)
    scale = jnp.exp(jax.random.uniform(key_scale, (N3, N1), jnp.float32) * spread)
    return noise * scale[None, :, None, :]


def scatter_about(own_key, dims, scale, reach, dtype=jnp.bfloat16):
    values = jax.random.normal(own_key, dims, jnp.float32) * scale
    return jnp.minimum(jnp.maximum(values, -reach), reach).astype(dtype)


def setup_inputs(seed: int = 0, part: int = 0) -> dict:
    keys = jax.random.split(jax.random.key(seed), 4)
    part_keys = jax.random.split(jax.random.fold_in(keys[3], part), 4)
    field = draw_field(jax.random.fold_in(jax.random.fold_in(keys[3], part), 71), part)
    start_x = scatter_about(keys[1], (N1, R1), 1.0, 6.0, jnp.float32)
    start_z = scatter_about(keys[2], (N3, R3), 1.0, 6.0, jnp.float32)
    return {"field": field, "start_x": start_x, "start_z": start_z}


def orthonormal(block):
    inner = jnp.dot(block.T, block, precision=lax.Precision.HIGHEST)
    lower = jnp.linalg.cholesky(inner)
    return lax.linalg.triangular_solve(lower, block, left_side=False, lower=True, transpose_a=True)

def subspace(gram, start):
    basis = start
    for sweep in range(SWEEPS):
        basis = orthonormal(jnp.dot(gram, basis, precision=lax.Precision.HIGHEST))
    return basis

def reference(field, start_x, start_z):
    flat = field.reshape(NT * N3 * N2, N1)
    gram_x = jnp.dot(flat.T, flat, precision=lax.Precision.HIGHEST)
    basis_x = subspace(gram_x, start_x)
    projected = jnp.einsum('tzyx,xr->rtzy', field, basis_x, precision=lax.Precision.HIGHEST)
    gram_z = jnp.einsum('rtzy,rtwy->zw', projected, projected, precision=lax.Precision.HIGHEST)
    basis_z = subspace(gram_z, start_z)
    core = jnp.einsum('rtzy,zs->rtsy', projected, basis_z, precision=lax.Precision.HIGHEST)
    return (core, basis_x, basis_z)
```

```python
import functools

import jax
import jax.numpy as jnp
from jax import lax
from jax.experimental import pallas as pl
from jax.experimental.pallas import tpu as pltpu
from jax.sharding import PartitionSpec as P

SWEEPS = 3
LANES = 128
MESH = pl.DeviceIdType.MESH
VMEM = pl.BlockSpec(memory_space=pltpu.VMEM)
LIMIT = 56 * 2**20


def params(**more):
    return pltpu.CompilerParams(vmem_limit_bytes=LIMIT, **more)


def split(x):
    high = x.astype(jnp.bfloat16)
    return high, (x - high.astype(jnp.float32)).astype(jnp.bfloat16)


def add_products(x, axis, sums):
    high, low = split(x)
    dims = (((axis,), (axis,)), ((), ()))
    sums[...] += lax.dot_general(
        high, jnp.concatenate([high, low], axis=1 - axis), dims, preferred_element_type=jnp.float32
    )


def pack(sums, out_ref):
    size = sums.shape[0]
    start = 0
    for block in range(size // LANES):
        first, depth = block * LANES, size - block * LANES
        columns, rows = pl.ds(first, LANES), pl.ds(first, depth)
        cross = sums[rows, pl.ds(size + first, LANES)] + sums[columns, pl.ds(size + first, depth)].T
        out_ref[pl.ds(start, depth), :] = sums[rows, columns] + cross
        start += depth
    if start < out_ref.shape[0]:
        out_ref[pl.ds(start, out_ref.shape[0] - start), :] = jnp.zeros((out_ref.shape[0] - start, LANES), jnp.float32)


def gram_kernel(axis, x_ref, out_ref, sums):
    @pl.when(pl.program_id(0) == 0)
    def _():
        sums[...] = jnp.zeros_like(sums)

    add_products(x_ref[...] if axis == 0 else x_ref[0], axis, sums)

    @pl.when(pl.program_id(0) == pl.num_programs(0) - 1)
    def _():
        pack(sums, out_ref)


def packed_rows(size, n):
    blocks = size // LANES
    rows = LANES * blocks * (blocks + 1) // 2
    unit = 16 * n
    return -(-rows // unit) * unit


def gram(x, axis, rows):
    size = x.shape[1]
    if axis == 0:
        step = min(1024, x.shape[0])
        grid, spec = x.shape[0] // step, pl.BlockSpec((step, size), lambda i: (i, 0))
    else:
        grid, spec = x.shape[0], pl.BlockSpec((1,) + x.shape[1:], lambda i: (i, 0, 0))
    return pl.pallas_call(
        functools.partial(gram_kernel, axis),
        grid=(grid,),
        in_specs=[spec],
        out_specs=pl.BlockSpec((rows, LANES), lambda i: (0, 0)),
        out_shape=jax.ShapeDtypeStruct((rows, LANES), jnp.float32),
        scratch_shapes=[pltpu.VMEM((size, 2 * size), jnp.float32)],
        compiler_params=params(),
    )(x)


def total_kernel(n, x_ref, out_ref, other, half, parts, pair, scatter, collect, back):
    g, c = lax.axis_index("gz"), lax.axis_index("ta")
    mate = {"ta": 1 - c}
    piece = parts.shape[1]
    depth = n * piece
    mine = pl.multiple_of(c * depth, 8)
    theirs = pl.multiple_of((1 - c) * depth, 8)

    def rows(base, k):
        return pl.ds(pl.multiple_of(base + k * piece, 8), piece)

    barrier = pltpu.get_barrier_semaphore()
    pl.semaphore_signal(barrier, inc=1, device_id=mate, device_id_type=MESH)

    @pl.loop(1, n)
    def _(i):
        pl.semaphore_signal(barrier, inc=1, device_id={"gz": lax.rem(g + i, n)}, device_id_type=MESH)

    pl.semaphore_wait(barrier, n)

    first = pltpu.make_async_remote_copy(
        x_ref.at[pl.ds(theirs, depth)], other, pair.at[0], pair.at[1], device_id=mate, device_id_type=MESH
    )
    first.start()
    first.wait()
    half[...] = x_ref[pl.ds(mine, depth), :] + other[...]

    def send(i):
        k = lax.rem(g + i, n)
        return pltpu.make_async_remote_copy(
            half.at[rows(0, k)], parts.at[i - 1], scatter.at[0, i], scatter.at[1, i], device_id={"gz": k}, device_id_type=MESH
        )

    def publish(i):
        k = lax.rem(g + i, n)
        own = out_ref.at[rows(mine, g)]
        return pltpu.make_async_remote_copy(
            own, own, collect.at[0, i], collect.at[1, i], device_id={"gz": k}, device_id_type=MESH
        )

    def forward(i):
        own = out_ref.at[rows(mine, lax.rem(g + n - i, n))]
        return pltpu.make_async_remote_copy(own, own, back.at[0, i], back.at[1, i], device_id=mate, device_id_type=MESH)

    @pl.loop(1, n)
    def _(i):
        send(i).start()

    @pl.loop(1, n)
    def _(i):
        send(i).wait_recv()

    out_ref[rows(mine, g), :] = half[rows(0, g), :] + jnp.sum(parts[...], axis=0)

    @pl.loop(1, n)
    def _(i):
        publish(i).start()

    forward(0).start()

    @pl.loop(1, n)
    def _(i):
        publish(i).wait_recv()
        forward(i).start()

    @pl.loop(0, n)
    def _(i):
        forward(i).wait()

    @pl.loop(1, n)
    def _(i):
        send(i).wait_send()
        publish(i).wait_send()


def total(x, n, collective_id):
    piece = x.shape[0] // (2 * n)
    dma = pltpu.SemaphoreType.DMA
    return pl.pallas_call(
        functools.partial(total_kernel, n),
        in_specs=[VMEM],
        out_specs=VMEM,
        out_shape=jax.ShapeDtypeStruct(x.shape, x.dtype),
        scratch_shapes=[
            pltpu.VMEM((n * piece, LANES), x.dtype),
            pltpu.VMEM((n * piece, LANES), x.dtype),
            pltpu.VMEM((n - 1, piece, LANES), x.dtype),
            dma((2,)),
            dma((2, n)),
            dma((2, n)),
            dma((2, n)),
        ],
        compiler_params=params(collective_id=collective_id, has_side_effects=True),
    )(x)


def exact(a, b, contract):
    return lax.dot_general(
        a, b, ((contract[:1], contract[1:]), ((), ())), precision=lax.Precision.HIGHEST, preferred_element_type=jnp.float32
    )


def inverse_factor(inner):
    r = inner.shape[0]
    row_id = lax.broadcasted_iota(jnp.int32, (r, 1), 0)
    eye = (lax.broadcasted_iota(jnp.int32, (r, r), 0) == lax.broadcasted_iota(jnp.int32, (r, r), 1)).astype(jnp.float32)
    work = jnp.concatenate([inner, eye], axis=1)
    tiles = [work[8 * t : 8 * t + 8] for t in range(r // 8)]
    local = lax.broadcasted_iota(jnp.int32, (8, 1), 0)
    for j in range(r):
        t0, s = divmod(j, 8)
        row = tiles[t0][s : s + 1]
        scaled = row * (1.0 / row[:, j : j + 1])
        if s < 7:
            factor = jnp.where(local > s, tiles[t0][:, j : j + 1], 0.0)
            updated = tiles[t0] - factor * scaled
        else:
            updated = tiles[t0]
        for t in range(t0 + 1, r // 8):
            tiles[t] = tiles[t] - tiles[t][:, j : j + 1] * scaled
        tiles[t0] = updated
    work = jnp.concatenate(tiles, axis=0)
    pivots = jnp.sum(work[:, :r] * eye, axis=1, keepdims=True)
    return work[:, r:] * (1.0 / jnp.sqrt(pivots))


def sweeps_kernel(g_ref, q_ref, out_ref, full):
    size = full.shape[0]
    start = 0
    for block in range(size // LANES):
        columns = pl.ds(block * LANES, LANES)
        full[pl.ds(block * LANES, size - block * LANES), columns] = g_ref[pl.ds(start, size - block * LANES), :]
        if block * LANES + LANES < size:
            below = pl.ds(block * LANES + LANES, size - block * LANES - LANES)
            full[columns, below] = g_ref[pl.ds(start + LANES, size - block * LANES - LANES), :].T
        start += size - block * LANES
    q = q_ref[...]
    for sweep in range(SWEEPS):
        z = exact(q, full[...], (1, 0))
        q = exact(inverse_factor(exact(z, z, (1, 1))), z, (1, 0))
    out_ref[...] = q


def subspace(packed, start_t):
    size = start_t.shape[1]
    return pl.pallas_call(
        sweeps_kernel,
        in_specs=[VMEM, VMEM],
        out_specs=VMEM,
        out_shape=jax.ShapeDtypeStruct(start_t.shape, jnp.float32),
        scratch_shapes=[pltpu.VMEM((size, size), jnp.float32)],
        compiler_params=params(),
    )(packed, start_t)


def body(n, field, start_x, start_z):
    flat = field.reshape(-1, field.shape[3])
    basis_x = subspace(total(gram(flat, 0, packed_rows(flat.shape[1], n)), n, 0), start_x.T)
    projected = jnp.einsum("tzyx,rx->rtzy", field, basis_x, precision=lax.Precision.HIGH)
    slab = lax.all_to_all(projected, "gz", split_axis=0, concat_axis=2, tiled=True)
    flat_slab = slab.reshape((-1,) + slab.shape[2:])
    basis_z = subspace(total(gram(flat_slab, 1, packed_rows(slab.shape[2], n)), n, 1), start_z.T)
    core = jnp.einsum("rtzy,sz->rtsy", slab, basis_z, precision=lax.Precision.HIGH)
    return (core, basis_x.T, basis_z.T)


def solution(mesh):
    in_specs = (P(("blocks", "ta"), "gz", None, None), P(), P())
    out_specs = (P(("blocks", "gz"), "ta", None, None), P("blocks", None), P("blocks", None))
    return jax.shard_map(
        functools.partial(body, mesh.shape["gz"]), mesh=mesh, in_specs=in_specs, out_specs=out_specs, check_vma=False
    )
```

```python
import functools

import jax
import jax.numpy as jnp
from jax import lax
from jax.experimental import pallas as pl
from jax.experimental.pallas import tpu as pltpu
from jax.sharding import PartitionSpec as P

SWEEPS = 3
LANES = 128
MESH = pl.DeviceIdType.MESH
VMEM = pl.BlockSpec(memory_space=pltpu.VMEM)
LIMIT = 56 * 2**20


def params(**more):
    return pltpu.CompilerParams(vmem_limit_bytes=LIMIT, **more)


def split(x):
    high = x.astype(jnp.bfloat16)
    return high, (x - high.astype(jnp.float32)).astype(jnp.bfloat16)


def add_products(x, axis, sums):
    high, low = split(x)
    dims = (((axis,), (axis,)), ((), ()))
    sums[...] += lax.dot_general(
        high, jnp.concatenate([high, low], axis=1 - axis), dims, preferred_element_type=jnp.float32
    )


def pack(sums, out_ref):
    size = sums.shape[0]
    start = 0
    for block in range(size // LANES):
        first, depth = block * LANES, size - block * LANES
        columns, rows = pl.ds(first, LANES), pl.ds(first, depth)
        cross = sums[rows, pl.ds(size + first, LANES)] + sums[columns, pl.ds(size + first, depth)].T
        out_ref[pl.ds(start, depth), :] = sums[rows, columns] + cross
        start += depth
    if start < out_ref.shape[0]:
        out_ref[pl.ds(start, out_ref.shape[0] - start), :] = jnp.zeros((out_ref.shape[0] - start, LANES), jnp.float32)


def gram_kernel(axis, x_ref, out_ref, sums):
    @pl.when(pl.program_id(0) == 0)
    def _():
        sums[...] = jnp.zeros_like(sums)

    add_products(x_ref[...] if axis == 0 else x_ref[0], axis, sums)

    @pl.when(pl.program_id(0) == pl.num_programs(0) - 1)
    def _():
        pack(sums, out_ref)


def packed_rows(size, n):
    blocks = size // LANES
    rows = LANES * blocks * (blocks + 1) // 2
    unit = 16 * n
    return -(-rows // unit) * unit


def gram(x, axis, rows):
    size = x.shape[1]
    if axis == 0:
        step = min(1024, x.shape[0])
        grid, spec = x.shape[0] // step, pl.BlockSpec((step, size), lambda i: (i, 0))
    else:
        grid, spec = x.shape[0], pl.BlockSpec((1,) + x.shape[1:], lambda i: (i, 0, 0))
    return pl.pallas_call(
        functools.partial(gram_kernel, axis),
        grid=(grid,),
        in_specs=[spec],
        out_specs=pl.BlockSpec((rows, LANES), lambda i: (0, 0)),
        out_shape=jax.ShapeDtypeStruct((rows, LANES), jnp.float32),
        scratch_shapes=[pltpu.VMEM((size, 2 * size), jnp.float32)],
        compiler_params=params(),
    )(x)


def total_kernel(n, x_ref, out_ref, other, half, parts, pair, scatter, collect, back):
    g, c = lax.axis_index("gz"), lax.axis_index("ta")
    mate = {"ta": 1 - c}
    piece = parts.shape[1]
    depth = n * piece
    mine = pl.multiple_of(c * depth, 8)
    theirs = pl.multiple_of((1 - c) * depth, 8)

    def rows(base, k):
        return pl.ds(pl.multiple_of(base + k * piece, 8), piece)

    barrier = pltpu.get_barrier_semaphore()
    pl.semaphore_signal(barrier, inc=1, device_id=mate, device_id_type=MESH)

    @pl.loop(1, n)
    def _(i):
        pl.semaphore_signal(barrier, inc=1, device_id={"gz": lax.rem(g + i, n)}, device_id_type=MESH)

    pl.semaphore_wait(barrier, n)

    first = pltpu.make_async_remote_copy(
        x_ref.at[pl.ds(theirs, depth)], other, pair.at[0], pair.at[1], device_id=mate, device_id_type=MESH
    )
    first.start()
    first.wait()
    half[...] = x_ref[pl.ds(mine, depth), :] + other[...]

    def send(i):
        k = lax.rem(g + i, n)
        return pltpu.make_async_remote_copy(
            half.at[rows(0, k)], parts.at[i - 1], scatter.at[0, i], scatter.at[1, i], device_id={"gz": k}, device_id_type=MESH
        )

    def publish(i):
        k = lax.rem(g + i, n)
        own = out_ref.at[rows(mine, g)]
        return pltpu.make_async_remote_copy(
            own, own, collect.at[0, i], collect.at[1, i], device_id={"gz": k}, device_id_type=MESH
        )

    def forward(i):
        own = out_ref.at[rows(mine, lax.rem(g + n - i, n))]
        return pltpu.make_async_remote_copy(own, own, back.at[0, i], back.at[1, i], device_id=mate, device_id_type=MESH)

    @pl.loop(1, n)
    def _(i):
        send(i).start()

    @pl.loop(1, n)
    def _(i):
        send(i).wait_recv()

    out_ref[rows(mine, g), :] = half[rows(0, g), :] + jnp.sum(parts[...], axis=0)

    @pl.loop(1, n)
    def _(i):
        publish(i).start()

    forward(0).start()

    @pl.loop(1, n)
    def _(i):
        publish(i).wait_recv()
        forward(i).start()

    @pl.loop(0, n)
    def _(i):
        forward(i).wait()

    @pl.loop(1, n)
    def _(i):
        send(i).wait_send()
        publish(i).wait_send()


def total(x, n, collective_id):
    piece = x.shape[0] // (2 * n)
    dma = pltpu.SemaphoreType.DMA
    return pl.pallas_call(
        functools.partial(total_kernel, n),
        in_specs=[VMEM],
        out_specs=VMEM,
        out_shape=jax.ShapeDtypeStruct(x.shape, x.dtype),
        scratch_shapes=[
            pltpu.VMEM((n * piece, LANES), x.dtype),
            pltpu.VMEM((n * piece, LANES), x.dtype),
            pltpu.VMEM((n - 1, piece, LANES), x.dtype),
            dma((2,)),
            dma((2, n)),
            dma((2, n)),
            dma((2, n)),
        ],
        compiler_params=params(collective_id=collective_id, has_side_effects=True),
    )(x)


def exact(a, b, contract):
    return lax.dot_general(
        a, b, ((contract[:1], contract[1:]), ((), ())), precision=lax.Precision.HIGHEST, preferred_element_type=jnp.float32
    )


def inverse_factor(inner):
    r = inner.shape[0]
    row_id = lax.broadcasted_iota(jnp.int32, (r, 1), 0)
    eye = (lax.broadcasted_iota(jnp.int32, (r, r), 0) == lax.broadcasted_iota(jnp.int32, (r, r), 1)).astype(jnp.float32)
    work = jnp.concatenate([inner, eye], axis=1)
    tiles = [work[8 * t : 8 * t + 8] for t in range(r // 8)]
    local = lax.broadcasted_iota(jnp.int32, (8, 1), 0)
    for j in range(r):
        t0, s = divmod(j, 8)
        row = tiles[t0][s : s + 1]
        scaled = row * (1.0 / row[:, j : j + 1])
        if s < 7:
            factor = jnp.where(local > s, tiles[t0][:, j : j + 1], 0.0)
            updated = tiles[t0] - factor * scaled
        else:
            updated = tiles[t0]
        for t in range(t0 + 1, r // 8):
            tiles[t] = tiles[t] - tiles[t][:, j : j + 1] * scaled
        tiles[t0] = updated
    work = jnp.concatenate(tiles, axis=0)
    pivots = jnp.sum(work[:, :r] * eye, axis=1, keepdims=True)
    return work[:, r:] * (1.0 / jnp.sqrt(pivots))


def sweeps_kernel(g_ref, q_ref, out_ref, full):
    size = full.shape[0]
    start = 0
    for block in range(size // LANES):
        columns = pl.ds(block * LANES, LANES)
        full[pl.ds(block * LANES, size - block * LANES), columns] = g_ref[pl.ds(start, size - block * LANES), :]
        if block * LANES + LANES < size:
            below = pl.ds(block * LANES + LANES, size - block * LANES - LANES)
            full[columns, below] = g_ref[pl.ds(start + LANES, size - block * LANES - LANES), :].T
        start += size - block * LANES
    q = q_ref[...]
    for sweep in range(SWEEPS):
        z = exact(q, full[...], (1, 0))
        q = exact(inverse_factor(exact(z, z, (1, 1))), z, (1, 0))
    out_ref[...] = q


def subspace(packed, start_t):
    size = start_t.shape[1]
    return pl.pallas_call(
        sweeps_kernel,
        in_specs=[VMEM, VMEM],
        out_specs=VMEM,
        out_shape=jax.ShapeDtypeStruct(start_t.shape, jnp.float32),
        scratch_shapes=[pltpu.VMEM((size, size), jnp.float32)],
        compiler_params=params(),
    )(packed, start_t)


def shuffle_kernel(n, field, w_ref, slab, packed, sent, chunks, sums, load, send_sem, recv_sem):
    g = lax.axis_index("gz")
    rank, depth = slab.shape[0], sent.shape[1]
    planes = chunks.shape[1]
    groups = depth // planes
    count = groups * (slab.shape[2] // LANES)
    at = pl.multiple_of(g * depth, 8)

    def place(c):
        plane = pl.multiple_of(lax.rem(c, groups) * planes, 8)
        return plane, pl.ds(pl.multiple_of(lax.div(c, groups) * LANES, LANES), LANES)

    def fetch(c):
        plane, columns = place(c)
        slot = lax.rem(c, 2)
        return pltpu.make_async_copy(field.at[pl.ds(plane, planes), columns, :], chunks.at[slot], load.at[slot])

    def ship(i, source, target, columns, half):
        k = lax.rem(g + i, n)
        return pltpu.make_async_remote_copy(
            sent.at[pl.ds(k * rank, rank), source, columns],
            slab.at[:, target, columns],
            send_sem.at[half, i],
            recv_sem.at[half, i],
            device_id={"gz": k},
            device_id_type=MESH,
        )

    fetch(0).start()
    barrier = pltpu.get_barrier_semaphore()

    @pl.loop(1, n)
    def _(i):
        pl.semaphore_signal(barrier, inc=1, device_id={"gz": lax.rem(g + i, n)}, device_id_type=MESH)

    w_high, w_low = split(w_ref[...])
    both = jnp.concatenate([w_high, w_low], axis=0)
    r = w_high.shape[0]
    dims = (((1,), (1,)), ((), ()))
    sums[...] = jnp.zeros_like(sums)
    pl.semaphore_wait(barrier, n - 1)

    @pl.loop(0, count)
    def _(c):
        @pl.when(c + 1 < count)
        def _():
            fetch(c + 1).start()

        fetch(c).wait()
        plane, columns = place(c)
        high, low = split(chunks[lax.rem(c, 2)].reshape(planes * LANES, chunks.shape[3]))
        first = lax.dot_general(both, high, dims, preferred_element_type=jnp.float32)
        second = lax.dot_general(w_high, low, dims, preferred_element_type=jnp.float32)
        sent[:, pl.ds(plane, planes), columns] = (first[:r] + first[r:] + second).reshape(r, planes, LANES)

        @pl.loop(1, n)
        def _(i):
            ship(
                i, pl.ds(plane, planes), pl.ds(pl.multiple_of(at + plane, 8), planes), columns, lax.div(c, groups)
            ).start()

    slab[:, pl.ds(at, depth), :] = sent[pl.ds(g * rank, rank)]

    @pl.loop(0, slab.shape[2] // LANES)
    def _(half):
        columns = pl.ds(pl.multiple_of(half * LANES, LANES), LANES)

        @pl.loop(1, n)
        def _(i):
            k = lax.rem(g + n - i, n)
            ship(i, pl.ds(0, depth), pl.ds(pl.multiple_of(k * depth, 8), depth), columns, half).wait_recv()

        @pl.loop(0, rank // 2)
        def _(pair):
            x = jnp.concatenate([slab[2 * pair, :, columns], slab[2 * pair + 1, :, columns]], axis=1)
            add_products(x, 1, sums)

    pack(sums, packed)

    @pl.loop(0, slab.shape[2] // LANES)
    def _(half):
        columns = pl.ds(pl.multiple_of(half * LANES, LANES), LANES)

        @pl.loop(1, n)
        def _(i):
            ship(i, pl.ds(0, depth), pl.ds(at, depth), columns, half).wait_send()


def shuffle(field, w, n, collective_id):
    depth, width, cells = field.shape
    r, size = w.shape[0], depth * n
    rows = packed_rows(size, n)
    dma = pltpu.SemaphoreType.DMA
    return pl.pallas_call(
        functools.partial(shuffle_kernel, n),
        in_specs=[pl.BlockSpec(memory_space=pl.ANY), VMEM],
        out_specs=[VMEM, VMEM],
        out_shape=[
            jax.ShapeDtypeStruct((r // n, size, width), jnp.float32),
            jax.ShapeDtypeStruct((rows, LANES), jnp.float32),
        ],
        scratch_shapes=[
            pltpu.VMEM((r, depth, width), jnp.float32),
            pltpu.VMEM((2, 8, LANES, cells), jnp.float32),
            pltpu.VMEM((size, 2 * size), jnp.float32),
            dma((2,)),
            dma((width // LANES, n)),
            dma((width // LANES, n)),
        ],
        compiler_params=params(collective_id=collective_id, has_side_effects=True),
    )(field, w)


def body(n, field, start_x, start_z):
    flat = field.reshape(-1, field.shape[3])
    basis_x = subspace(total(gram(flat, 0, packed_rows(flat.shape[1], n)), n, 0), start_x.T)
    slab, packed = shuffle(field[0], basis_x, n, 2)
    basis_z = subspace(total(packed, n, 1), start_z.T)
    core = jnp.einsum("rzy,sz->rsy", slab, basis_z, precision=lax.Precision.HIGH)[:, None]
    return (core, basis_x.T, basis_z.T)


def solution(mesh):
    in_specs = (P(("blocks", "ta"), "gz", None, None), P(), P())
    out_specs = (P(("blocks", "gz"), "ta", None, None), P("blocks", None), P("blocks", None))
    return jax.shard_map(
        functools.partial(body, mesh.shape["gz"]), mesh=mesh, in_specs=in_specs, out_specs=out_specs, check_vma=False
    )
```

```python
import functools

import jax
import jax.numpy as jnp
from jax import lax
from jax.experimental import pallas as pl
from jax.experimental.pallas import tpu as pltpu
from jax.sharding import PartitionSpec as P

SWEEPS = 3
LANES = 128
STEP = 8
MESH = pl.DeviceIdType.MESH
VMEM = pl.BlockSpec(memory_space=pltpu.VMEM)
LIMIT = 56 * 2**20


def params(**more):
    return pltpu.CompilerParams(vmem_limit_bytes=LIMIT, **more)


def split(x):
    high = x.astype(jnp.bfloat16)
    return high, (x - high.astype(jnp.float32)).astype(jnp.bfloat16)


def add_products(x, axis, sums):
    high, low = split(x)
    dims = (((axis,), (axis,)), ((), ()))
    sums[...] += lax.dot_general(
        high, jnp.concatenate([high, low], axis=1 - axis), dims, preferred_element_type=jnp.float32
    )


def pack(sums, out_ref):
    size = sums.shape[0]
    start = 0
    for block in range(size // LANES):
        first, depth = block * LANES, size - block * LANES
        columns, rows = pl.ds(first, LANES), pl.ds(first, depth)
        cross = sums[rows, pl.ds(size + first, LANES)] + sums[columns, pl.ds(size + first, depth)].T
        out_ref[pl.ds(start, depth), :] = sums[rows, columns] + cross
        start += depth
    if start < out_ref.shape[0]:
        out_ref[pl.ds(start, out_ref.shape[0] - start), :] = jnp.zeros((out_ref.shape[0] - start, LANES), jnp.float32)


def gram_kernel(axis, x_ref, out_ref, sums):
    @pl.when(pl.program_id(0) == 0)
    def _():
        sums[...] = jnp.zeros_like(sums)

    add_products(x_ref[...] if axis == 0 else x_ref[0], axis, sums)

    @pl.when(pl.program_id(0) == pl.num_programs(0) - 1)
    def _():
        pack(sums, out_ref)


def packed_rows(size, n):
    blocks = size // LANES
    rows = LANES * blocks * (blocks + 1) // 2
    unit = 16 * n
    return -(-rows // unit) * unit


def gram(x, axis, rows):
    size = x.shape[1]
    if axis == 0:
        step = min(2048, x.shape[0])
        grid, spec = x.shape[0] // step, pl.BlockSpec((step, size), lambda i: (i, 0))
    else:
        grid, spec = x.shape[0], pl.BlockSpec((1,) + x.shape[1:], lambda i: (i, 0, 0))
    return pl.pallas_call(
        functools.partial(gram_kernel, axis),
        grid=(grid,),
        in_specs=[spec],
        out_specs=pl.BlockSpec((rows, LANES), lambda i: (0, 0)),
        out_shape=jax.ShapeDtypeStruct((rows, LANES), jnp.float32),
        scratch_shapes=[pltpu.VMEM((size, 2 * size), jnp.float32)],
        compiler_params=params(),
    )(x)


def total_kernel(n, x_ref, out_ref, other, half, parts, pair, scatter, collect, back):
    g, c = lax.axis_index("gz"), lax.axis_index("ta")
    mate = {"ta": 1 - c}
    piece = parts.shape[1]
    depth = n * piece
    mine = pl.multiple_of(c * depth, 8)
    theirs = pl.multiple_of((1 - c) * depth, 8)

    def rows(base, k):
        return pl.ds(pl.multiple_of(base + k * piece, 8), piece)

    barrier = pltpu.get_barrier_semaphore()
    pl.semaphore_signal(barrier, inc=1, device_id=mate, device_id_type=MESH)

    @pl.loop(1, n)
    def _(i):
        pl.semaphore_signal(barrier, inc=1, device_id={"gz": lax.rem(g + i, n)}, device_id_type=MESH)

    pl.semaphore_wait(barrier, n)

    first = pltpu.make_async_remote_copy(
        x_ref.at[pl.ds(theirs, depth)], other, pair.at[0], pair.at[1], device_id=mate, device_id_type=MESH
    )
    first.start()
    first.wait()
    half[...] = x_ref[pl.ds(mine, depth), :] + other[...]

    def send(i):
        k = lax.rem(g + i, n)
        return pltpu.make_async_remote_copy(
            half.at[rows(0, k)], parts.at[i - 1], scatter.at[0, i], scatter.at[1, i], device_id={"gz": k}, device_id_type=MESH
        )

    def publish(i):
        k = lax.rem(g + i, n)
        own = out_ref.at[rows(mine, g)]
        return pltpu.make_async_remote_copy(
            own, own, collect.at[0, i], collect.at[1, i], device_id={"gz": k}, device_id_type=MESH
        )

    def forward(i):
        own = out_ref.at[rows(mine, lax.rem(g + n - i, n))]
        return pltpu.make_async_remote_copy(own, own, back.at[0, i], back.at[1, i], device_id=mate, device_id_type=MESH)

    @pl.loop(1, n)
    def _(i):
        send(i).start()

    @pl.loop(1, n)
    def _(i):
        send(i).wait_recv()

    out_ref[rows(mine, g), :] = half[rows(0, g), :] + jnp.sum(parts[...], axis=0)

    @pl.loop(1, n)
    def _(i):
        publish(i).start()

    forward(0).start()

    @pl.loop(1, n)
    def _(i):
        publish(i).wait_recv()
        forward(i).start()

    @pl.loop(0, n)
    def _(i):
        forward(i).wait()

    @pl.loop(1, n)
    def _(i):
        send(i).wait_send()
        publish(i).wait_send()


def total(x, n, collective_id):
    piece = x.shape[0] // (2 * n)
    dma = pltpu.SemaphoreType.DMA
    return pl.pallas_call(
        functools.partial(total_kernel, n),
        in_specs=[VMEM],
        out_specs=VMEM,
        out_shape=jax.ShapeDtypeStruct(x.shape, x.dtype),
        scratch_shapes=[
            pltpu.VMEM((n * piece, LANES), x.dtype),
            pltpu.VMEM((n * piece, LANES), x.dtype),
            pltpu.VMEM((n - 1, piece, LANES), x.dtype),
            dma((2,)),
            dma((2, n)),
            dma((2, n)),
            dma((2, n)),
        ],
        compiler_params=params(collective_id=collective_id, has_side_effects=True),
    )(x)


def exact(a, b, contract):
    return lax.dot_general(
        a, b, ((contract[:1], contract[1:]), ((), ())), precision=lax.Precision.HIGHEST, preferred_element_type=jnp.float32
    )


def inverse_factor(inner):
    r = inner.shape[0]
    row_id = lax.broadcasted_iota(jnp.int32, (r, 1), 0)
    eye = (lax.broadcasted_iota(jnp.int32, (r, r), 0) == lax.broadcasted_iota(jnp.int32, (r, r), 1)).astype(jnp.float32)
    work = jnp.concatenate([inner, eye], axis=1)
    tiles = [work[8 * t : 8 * t + 8] for t in range(r // 8)]
    local = lax.broadcasted_iota(jnp.int32, (8, 1), 0)
    def spread(x):
        return jnp.broadcast_to(x, (8, 2 * r))

    for j in range(0, r, STEP):
        t0, s = divmod(j, 8)
        upper = [[spread(tiles[t0][s + k : s + k + 1, j + m : j + m + 1]) for m in range(STEP)] for k in range(STEP)]
        rows = [spread(tiles[t0][s + k : s + k + 1]) for k in range(STEP)]
        columns = [[spread(tile[:, j + k : j + k + 1]) for k in range(STEP)] for tile in tiles[t0:]]
        inverse, ratio = [], []
        for k in range(STEP):
            inverse.append(1.0 / upper[k][k])
            ratio.append([upper[k][m] * inverse[k] for m in range(STEP)])
            for q in range(k + 1, STEP):
                rows[q] = rows[q] - ratio[k][q] * rows[k]
                for m in range(q, STEP):
                    upper[q][m] = upper[q][m] - ratio[k][q] * upper[k][m]
        scaled = [rows[k] * inverse[k] for k in range(STEP)]
        for t in range(t0, r // 8):
            own = columns[t - t0]
            for k in range(STEP):
                for q in range(k + 1, STEP):
                    own[q] = own[q] - own[k] * ratio[k][q]
                factor = jnp.where(local > s + k, own[k], 0.0) if t == t0 else own[k]
                tiles[t] = tiles[t] - factor * scaled[k]
    work = jnp.concatenate(tiles, axis=0)
    pivots = jnp.sum(work[:, :r] * eye, axis=1, keepdims=True)
    return work[:, r:] * (1.0 / jnp.sqrt(pivots))


def sweeps_kernel(g_ref, q_ref, out_ref, full):
    size = full.shape[0]
    start = 0
    for block in range(size // LANES):
        columns = pl.ds(block * LANES, LANES)
        full[pl.ds(block * LANES, size - block * LANES), columns] = g_ref[pl.ds(start, size - block * LANES), :]
        if block * LANES + LANES < size:
            below = pl.ds(block * LANES + LANES, size - block * LANES - LANES)
            full[columns, below] = g_ref[pl.ds(start + LANES, size - block * LANES - LANES), :].T
        start += size - block * LANES
    q = q_ref[...]
    for sweep in range(SWEEPS):
        z = exact(q, full[...], (1, 0))
        q = exact(inverse_factor(exact(z, z, (1, 1))), z, (1, 0))
    out_ref[...] = q


def subspace(packed, start_t):
    size = start_t.shape[1]
    return pl.pallas_call(
        sweeps_kernel,
        in_specs=[VMEM, VMEM],
        out_specs=VMEM,
        out_shape=jax.ShapeDtypeStruct(start_t.shape, jnp.float32),
        scratch_shapes=[pltpu.VMEM((size, size), jnp.float32)],
        compiler_params=params(),
    )(packed, start_t)


def shuffle_kernel(n, field, w_ref, slab, packed, sent, chunks, sums, load, send_sem, recv_sem):
    g = lax.axis_index("gz")
    rank, depth = slab.shape[0], sent.shape[1]
    planes = chunks.shape[1]
    groups = depth // planes
    count = groups * (slab.shape[2] // LANES)
    at = pl.multiple_of(g * depth, 8)

    def place(c):
        plane = pl.multiple_of(lax.rem(c, groups) * planes, 8)
        return plane, pl.ds(pl.multiple_of(lax.div(c, groups) * LANES, LANES), LANES)

    def fetch(c):
        plane, columns = place(c)
        slot = lax.rem(c, 2)
        return pltpu.make_async_copy(field.at[pl.ds(plane, planes), columns, :], chunks.at[slot], load.at[slot])

    def ship(i, source, target, columns, half):
        k = lax.rem(g + i, n)
        return pltpu.make_async_remote_copy(
            sent.at[pl.ds(k * rank, rank), source, columns],
            slab.at[:, target, columns],
            send_sem.at[half, i],
            recv_sem.at[half, i],
            device_id={"gz": k},
            device_id_type=MESH,
        )

    fetch(0).start()
    barrier = pltpu.get_barrier_semaphore()

    @pl.loop(1, n)
    def _(i):
        pl.semaphore_signal(barrier, inc=1, device_id={"gz": lax.rem(g + i, n)}, device_id_type=MESH)

    w_high, w_low = split(w_ref[...])
    both = jnp.concatenate([w_high, w_low], axis=0)
    r = w_high.shape[0]
    dims = (((1,), (1,)), ((), ()))
    sums[...] = jnp.zeros_like(sums)
    pl.semaphore_wait(barrier, n - 1)

    @pl.loop(0, count)
    def _(c):
        @pl.when(c + 1 < count)
        def _():
            fetch(c + 1).start()

        fetch(c).wait()
        plane, columns = place(c)
        high, low = split(chunks[lax.rem(c, 2)].reshape(planes * LANES, chunks.shape[3]))
        first = lax.dot_general(both, high, dims, preferred_element_type=jnp.float32)
        second = lax.dot_general(w_high, low, dims, preferred_element_type=jnp.float32)
        sent[:, pl.ds(plane, planes), columns] = (first[:r] + first[r:] + second).reshape(r, planes, LANES)

        @pl.loop(1, n)
        def _(i):
            ship(
                i, pl.ds(plane, planes), pl.ds(pl.multiple_of(at + plane, 8), planes), columns, lax.div(c, groups)
            ).start()

    slab[:, pl.ds(at, depth), :] = sent[pl.ds(g * rank, rank)]

    @pl.loop(0, slab.shape[2] // LANES)
    def _(half):
        columns = pl.ds(pl.multiple_of(half * LANES, LANES), LANES)

        @pl.loop(1, n)
        def _(i):
            k = lax.rem(g + n - i, n)
            ship(i, pl.ds(0, depth), pl.ds(pl.multiple_of(k * depth, 8), depth), columns, half).wait_recv()

        @pl.loop(0, rank // 2)
        def _(pair):
            x = jnp.concatenate([slab[2 * pair, :, columns], slab[2 * pair + 1, :, columns]], axis=1)
            add_products(x, 1, sums)

    pack(sums, packed)

    @pl.loop(0, slab.shape[2] // LANES)
    def _(half):
        columns = pl.ds(pl.multiple_of(half * LANES, LANES), LANES)

        @pl.loop(1, n)
        def _(i):
            ship(i, pl.ds(0, depth), pl.ds(at, depth), columns, half).wait_send()


def shuffle(field, w, n, collective_id):
    depth, width, cells = field.shape
    r, size = w.shape[0], depth * n
    rows = packed_rows(size, n)
    dma = pltpu.SemaphoreType.DMA
    return pl.pallas_call(
        functools.partial(shuffle_kernel, n),
        in_specs=[pl.BlockSpec(memory_space=pl.ANY), VMEM],
        out_specs=[VMEM, VMEM],
        out_shape=[
            jax.ShapeDtypeStruct((r // n, size, width), jnp.float32),
            jax.ShapeDtypeStruct((rows, LANES), jnp.float32),
        ],
        scratch_shapes=[
            pltpu.VMEM((r, depth, width), jnp.float32),
            pltpu.VMEM((2, 8, LANES, cells), jnp.float32),
            pltpu.VMEM((size, 2 * size), jnp.float32),
            dma((2,)),
            dma((width // LANES, n)),
            dma((width // LANES, n)),
        ],
        compiler_params=params(collective_id=collective_id, has_side_effects=True),
    )(field, w)


def body(n, field, start_x, start_z):
    flat = field.reshape(-1, field.shape[3])
    basis_x = subspace(total(gram(flat, 0, packed_rows(flat.shape[1], n)), n, 0), start_x.T)
    slab, packed = shuffle(field[0], basis_x, n, 2)
    basis_z = subspace(total(packed, n, 1), start_z.T)
    core = jnp.einsum("rzy,sz->rsy", slab, basis_z, precision=lax.Precision.HIGH)[:, None]
    return (core, basis_x.T, basis_z.T)


def solution(mesh):
    in_specs = (P(("blocks", "ta"), "gz", None, None), P(), P())
    out_specs = (P(("blocks", "gz"), "ta", None, None), P("blocks", None), P("blocks", None))
    return jax.shard_map(
        functools.partial(body, mesh.shape["gz"]), mesh=mesh, in_specs=in_specs, out_specs=out_specs, check_vma=False
    )
```
